512 devices in a mesh: tm: 32 (over z, y_hi, core), space: 16 (over x, y_lo).
Axes of the slice: x: 4, y: 8 (y_hi: 2, y_lo: 4; y = y_hi * 4 + y_lo), z: 8, core: 2. Of those that a mesh axis runs over, the one named last changes fastest.
Arguments:
- q_spatial: bfloat16 [64, 1024, 1152], P('tm', 'space'), may hold values from -40 to 40
- k_spatial: bfloat16 [64, 1024, 1152], P('tm', 'space'), may hold values from -40 to 40
- v_spatial: bfloat16 [64, 1024, 1152], P('tm', 'space'), may hold values from -6 to 6
- stream: bfloat16 [64, 1024, 1152], P('tm', 'space'), may hold values from -6 to 6
- q_temporal: bfloat16 [64, 1024, 1152], P('tm', 'space'), may hold values from -40 to 40
- k_temporal: bfloat16 [64, 1024, 1152], P('tm', 'space'), may hold values from -40 to 40
Outputs:
- spatial_out: bfloat16 [64, 1024, 1152], P('tm', 'space')
- temporal_out: bfloat16 [64, 1024, 1152], P('tm', 'space')
The draws below stay inside these ranges and needn't reach their ends.
All inputs are finite; a program needn't handle non-finite values.
Results may differ from the reference program's by a relative error of at most 0.0053.
Values may be sent and summed in bfloat16 or wider, within the bound.
A program may use at most 64 MiB of HBM per device.

```python
import jax
import jax.numpy as jnp
from jax import lax

D = 1152
HEADS = 16
SEQ = 1024
FRAMES = 64


def paired_draw(key):
    full_shape = (FRAMES, SEQ, D)
    key_rows = jax.random.normal(jax.random.fold_in(key, 1), full_shape, jnp.float32) * 1.7
    queries = jax.random.normal(jax.random.fold_in(key, 2), full_shape, jnp.float32) * 1.7
    queries = jnp.clip(queries, -40.0, 40.0)
    key_rows = jnp.clip(key_rows, -40.0, 40.0)
    return (queries, key_rows)


def draw_q_spatial(key, part):
    return paired_draw(jax.random.fold_in(key, 11))[0].astype(jnp.bfloat16)


def draw_k_spatial(key, part):
    return paired_draw(jax.random.fold_in(key, 11))[1].astype(jnp.bfloat16)


def draw_q_temporal(key, part):
    return paired_draw(jax.random.fold_in(key, 23))[0].astype(jnp.bfloat16)


def draw_k_temporal(key, part):
    return paired_draw(jax.random.fold_in(key, 23))[1].astype(jnp.bfloat16)


def steps_of(key, shape, cuts, low, largest):
    gain = 1.0
    for dim, shards_of in cuts:
        draws = jax.random.uniform(jax.random.fold_in(jax.random.fold_in(key, 6), dim), (shards_of,), jnp.float32, low / len(cuts), largest / len(cuts))
        gain = gain * jnp.repeat(jnp.exp(draws), shape[dim] // shards_of).reshape((-1,) + (1,) * (len(shape) - 1 - dim))
    return gain


def centred(own_key, shape, deviation, most, shards=(), kind=jnp.bfloat16):
    values = deviation * jax.random.normal(own_key, shape, jnp.float32)
    if shards:
        values = values * steps_of(own_key, shape, shards, -0.22, 0.18)
    return jnp.clip(values, -most, most).astype(kind)


def setup_inputs(seed: int = 0) -> dict:
    key_of = jax.random.split(jax.random.key(seed), 7)
    return {
        "q_spatial": draw_q_spatial(jax.random.fold_in(key_of[6], 71), 0),
        "k_spatial": draw_k_spatial(jax.random.fold_in(key_of[6], 71), 0),
        "v_spatial": centred(key_of[2], (FRAMES, SEQ, D), 1.0, 6.0, ((0, 32), (1, 16))),
        "stream": centred(key_of[3], (FRAMES, SEQ, D), 1.0, 6.0, ((0, 32), (1, 16))),
        "q_temporal": draw_q_temporal(jax.random.fold_in(key_of[6], 71), 0),
        "k_temporal": draw_k_temporal(jax.random.fold_in(key_of[6], 71), 0),
    }


def head_attention(queries, key_rows, value_rows):
    length = queries.shape[0]
    head_size = queries.shape[1]
    score_scale = 1.0 / (head_size ** 0.5)
    q_size = 512 if length % 512 == 0 else length
    blocked = queries.reshape(length // q_size, q_size, head_size)

    def one_block(q_block):
        scores = jnp.dot(q_block, key_rows.T, preferred_element_type=jnp.float32) * score_scale
        maxima = jnp.max(scores, axis=-1, keepdims=True)
        raised = jnp.exp(scores - maxima)
        totals = jnp.sum(raised, axis=-1)
        mixed = jnp.dot(raised.astype(jnp.bfloat16), value_rows, preferred_element_type=jnp.float32)
        return mixed / totals[:, None]

    return lax.map(one_block, blocked).reshape(length, head_size)


def frame_attention(triple):
    queries, key_rows, value_rows = triple
    length = queries.shape[0]
    head_size = D // HEADS
    def split(arr):
        return jnp.moveaxis(arr.reshape(length, HEADS, head_size), 1, 0)
    mixed = lax.map(lambda tri: head_attention(tri[0], tri[1], tri[2]), (split(queries), split(key_rows), split(value_rows)))
    return jnp.moveaxis(mixed, 0, 1).reshape(length, D).astype(jnp.bfloat16)


def reference(q_spatial, k_spatial, v_spatial, stream, q_temporal, k_temporal):
    spatial_out = lax.map(frame_attention, (q_spatial, k_spatial, v_spatial))
    values_t = (stream.astype(jnp.float32) + spatial_out.astype(jnp.float32)).astype(jnp.bfloat16)
    head_size = D // HEADS
    score_scale = 1.0 / (head_size ** 0.5)
    def split(arr):
        return jnp.moveaxis(arr.reshape(FRAMES, SEQ, HEADS, head_size), 2, 0)

    def one_head(triple):
        queries, key_rows, value_rows = triple
        scores = jnp.einsum('fsd,gsd->sfg', queries.astype(jnp.float32), key_rows.astype(jnp.float32)) * score_scale
        maxima = jnp.max(scores, axis=-1, keepdims=True)
        raised = jnp.exp(scores - maxima)
        totals = jnp.sum(raised, axis=-1)
        mixed = jnp.einsum('sfg,gsd->fsd', raised.astype(jnp.bfloat16).astype(jnp.float32), value_rows.astype(jnp.float32))
        return mixed / jnp.transpose(totals)[:, :, None]

    mixed = lax.map(one_head, (split(q_temporal), split(k_temporal), split(values_t)))
    temporal_out = jnp.moveaxis(mixed, 0, 2).reshape(FRAMES, SEQ, D).astype(jnp.bfloat16)
    return spatial_out, temporal_out
```

```python
import math

import jax
import jax.numpy as jnp
from jax import lax
from jax.experimental import pallas as pl
from jax.experimental.pallas import tpu as pltpu
from jax.sharding import PartitionSpec as P

D = 1152
HEADS = 16
HS = 72
LT = 9
NS = 16
NT = 32
BF = jnp.bfloat16
F32 = jnp.float32
MESH = pl.DeviceIdType.MESH
FACTOR = math.log2(math.e) / math.sqrt(HS)


def dot(a, b):
    return lax.dot_general(a, b, (((1,), (0,)), ((), ())), preferred_element_type=F32)


def dot_nt(a, b):
    return lax.dot_general(a, b, (((1,), (1,)), ((), ())), preferred_element_type=F32)


def one_hot(n, column_of_row):
    rows = lax.broadcasted_iota(jnp.int32, (n, n), 0)
    cols = lax.broadcasted_iota(jnp.int32, (n, n), 1)
    return jnp.where(cols == column_of_row(rows), 1.0, 0.0).astype(BF)


def one_hot_t(n, row_of_column):
    rows = lax.broadcasted_iota(jnp.int32, (n, n), 0)
    cols = lax.broadcasted_iota(jnp.int32, (n, n), 1)
    return jnp.where(rows == row_of_column(cols), 1.0, 0.0).astype(BF)


def bits(r, low, count):
    return (r >> low) & ((1 << count) - 1)


def frame_major(r):
    return bits(r, 6, 1) * 128 + bits(r, 7, 1) * 64 + bits(r, 0, 6)


def by_peer(r):
    return bits(r, 2, 1) * 128 + bits(r, 1, 1) * 64 + bits(r, 3, 5) * 2 + bits(r, 0, 1)


def by_position(r):
    return bits(r, 1, 5) * 8 + bits(r, 7, 1) * 4 + bits(r, 0, 1) * 2 + bits(r, 6, 1)


def kernel(
    q_ref, k_ref, v_ref, stream_ref, qt_ref, kt_ref, spatial_ref, temporal_ref,
    xt, rs, osend, orecv, qks, qkr, vs, vr, ts, tr, q_f, k_f, v_f, q_p, k_p, v_p, o_p,
    send_x, recv_x, send_o, recv_o, send_qk, recv_qk, send_v, recv_v, send_t, recv_t, local,
):
    s = lax.axis_index("space")
    t = lax.axis_index("tm")

    barrier = pltpu.get_barrier_semaphore()

    def greet_space(i, c):
        pl.semaphore_signal(barrier, inc=1, device_id={"space": lax.rem(s + i, NS)}, device_id_type=MESH)
        return c

    def greet_tm(i, c):
        pl.semaphore_signal(barrier, inc=1, device_id={"tm": lax.rem(t + i, NT)}, device_id_type=MESH)
        return c

    lax.fori_loop(1, NS, greet_space, 0)
    lax.fori_loop(1, NT, greet_tm, 0)

    eye = one_hot(128, lambda r: r)

    for a, ref in enumerate((q_ref, k_ref, v_ref)):
        for j in range(LT):
            block = ref[:, :, 128 * j : 128 * j + 128].reshape(128, 128)
            xt[a, 16 * j : 16 * j + 16] = dot_nt(eye, block).reshape(16, 8, 128).astype(BF)

    pl.semaphore_wait(barrier, NS + NT - 2)

    def space_x(p, at):
        return pltpu.make_async_remote_copy(
            src_ref=xt.at[:, pl.ds(9 * p, 9)], dst_ref=rs.at[at], send_sem=send_x.at[p], recv_sem=recv_x.at[at],
            device_id={"space": p}, device_id_type=MESH)

    def tm_copy(src, dst, send, recv, p, at):
        return pltpu.make_async_remote_copy(
            src_ref=src.at[p], dst_ref=dst.at[at], send_sem=send.at[p], recv_sem=recv.at[at],
            device_id={"tm": p}, device_id_type=MESH)

    def tm_start(src, dst, send, recv):
        def body(i, c):
            tm_copy(src, dst, send, recv, lax.rem(t + i, NT), t).start()
            return c

        lax.fori_loop(1, NT, body, 0)
        own = pltpu.make_async_copy(src.at[t], dst.at[t], recv.at[t])
        own.start()

    def tm_wait(src, dst, send, recv):
        def body(i, c):
            p = lax.rem(t + i, NT)
            tm_copy(src, dst, send, recv, p, p).wait()
            return c

        lax.fori_loop(1, NT, body, 0)
        pltpu.make_async_copy(src.at[t], dst.at[t], recv.at[t]).wait()

    def start_x(i, c):
        space_x(lax.rem(s + i, NS), s).start()
        return c

    lax.fori_loop(1, NS, start_x, 0)
    own_x = pltpu.make_async_copy(xt.at[:, pl.ds(9 * s, 9)], rs.at[s], local)
    own_x.start()

    to_peer = one_hot(256, by_peer)
    for j in range(LT):
        pair = jnp.concatenate(
            [ref[:, :, 128 * j : 128 * j + 128].reshape(128, 128) for ref in (qt_ref, kt_ref)], axis=0
        )
        qks[:, j] = dot(to_peer, pair).reshape(32, 8, 128).astype(BF)
    tm_start(qks, qkr, send_qk, recv_qk)

    own_x.wait()

    def wait_x(i, c):
        p = lax.rem(s + i, NS)
        space_x(p, p).wait()
        return c

    lax.fori_loop(1, NS, wait_x, 0)

    sort = one_hot_t(256, frame_major)
    sort_t = one_hot(256, frame_major)
    for i in range(NS // 2):
        pair = [rs[2 * i + m].reshape(216, 128) for m in range(2)]
        pair = jnp.concatenate(pair, axis=1)
        qv = dot(pair, sort)
        keys = dot_nt(sort_t, pair[HS : 2 * HS])
        for f in range(2):
            q_f[f, :HS, 128 * i : 128 * i + 128] = qv[:HS, 128 * f : 128 * f + 128].astype(BF)
            v_f[f, :HS, 128 * i : 128 * i + 128] = qv[2 * HS :, 128 * f : 128 * f + 128].astype(BF)
            k_f[f, 128 * i : 128 * i + 128, :HS] = keys[128 * f : 128 * f + 128].astype(BF)

    def copy_o(p, at):
        return pltpu.make_async_remote_copy(
            src_ref=osend.at[p], dst_ref=orecv.at[at], send_sem=send_o.at[p], recv_sem=recv_o.at[at],
            device_id={"space": p}, device_id_type=MESH)

    own_o = pltpu.make_async_copy(osend.at[s], orecv.at[s], local)

    def attend(i, c):
        tile = lax.rem(lax.div(s, 4) + i, 4)
        at = pl.ds(pl.multiple_of(tile * 256, 256), 256)
        mixed = []
        for f in range(2):
            scores = dot(k_f[f, :, :HS], q_f[f, :HS, at])
            top = jnp.max(scores, axis=0, keepdims=True) * FACTOR
            raised = jnp.exp2(scores * FACTOR - top)
            total = jnp.sum(raised, axis=0, keepdims=True)
            mix = dot(v_f[f, :HS, :], raised.astype(BF))
            mixed.append((mix / total).astype(BF))
        for m in range(2):
            back = dot(jnp.concatenate([x[:, 128 * m : 128 * m + 128] for x in mixed], axis=1), sort_t)
            for n in range(2):
                osend[4 * tile + 2 * m + n] = back[:, 128 * n : 128 * n + 128].reshape(9, 8, 128).astype(BF)
        for n in range(4):
            p = 4 * tile + n

            @pl.when(p != s)
            def _():
                copy_o(p, s).start()

            @pl.when(p == s)
            def _():
                own_o.start()

        return c

    lax.fori_loop(0, 4, attend, 0)

    def wait_o(i, c):
        p = lax.rem(s + i, NS)
        copy_o(p, p).wait()
        return c

    own_o.wait()
    lax.fori_loop(1, NS, wait_o, 0)

    zeros = jnp.zeros((128, 128), BF)
    for j in range(5):
        pair = []
        for n in (2 * j, 2 * j + 1):
            if n == LT:
                pair.append(zeros)
                continue
            rows = [orecv[r // 9, r % 9] for r in range(16 * n, 16 * n + 16)]
            block = dot_nt(eye, jnp.concatenate(rows, axis=0)).astype(BF)
            lanes = slice(128 * n, 128 * n + 128)
            spatial_ref[:, :, lanes] = block.reshape(2, 64, 128)
            stream = stream_ref[:, :, lanes].reshape(128, 128)
            pair.append((stream.astype(F32) + block.astype(F32)).astype(BF))
        vs[:, j] = dot(to_peer, jnp.concatenate(pair, axis=0)).reshape(32, 8, 128).astype(BF)
    tm_start(vs, vr, send_v, recv_v)

    tm_wait(qks, qkr, send_qk, recv_qk)
    to_position = one_hot(256, by_position)
    for j in range(LT):
        both = dot(to_position, qkr[:, j].reshape(256, 128)).astype(BF)
        q_p[:, 128 * j : 128 * j + 128] = both[:128]
        k_p[:, 128 * j : 128 * j + 128] = both[128:]
    tm_wait(vs, vr, send_v, recv_v)
    for j in range(5):
        both = dot(to_position, vr[:, j].reshape(256, 128)).astype(BF)
        for n in range(2):
            if 2 * j + n < LT:
                v_p[:, 128 * (2 * j + n) : 128 * (2 * j + n) + 128] = both[128 * n : 128 * n + 128]

    rows = lax.broadcasted_iota(jnp.int32, (128, 128), 0)
    cols = lax.broadcasted_iota(jnp.int32, (128, 128), 1)
    same = (rows >> 6) == (cols >> 6)
    for h in range(HEADS):
        low, high = HS * h // 128 * 128, -(-HS * (h + 1) // 128) * 128
        lane = lax.broadcasted_iota(jnp.int32, (128, high - low), 1) + low
        mine = (lane >= HS * h) & (lane < HS * (h + 1))
        keys = jnp.where(mine, k_p[:, low:high].astype(F32), 0.0).astype(BF)
        scores = jnp.where(same, dot_nt(q_p[:, low:high], keys), -jnp.inf)
        top = jnp.max(scores, axis=1, keepdims=True) * FACTOR
        raised = jnp.exp2(scores * FACTOR - top)
        total = jnp.sum(raised, axis=1, keepdims=True)
        mix = dot(raised.astype(BF), v_p[:, low:high]) / total
        o_p[:, low:high] = jnp.where(mine, mix, o_p[:, low:high])

    from_position = one_hot_t(256, by_position)
    for j in range(5):
        pair = [o_p[:, 128 * n : 128 * n + 128].astype(BF) if n < LT else zeros for n in (2 * j, 2 * j + 1)]
        ts[:, j] = dot(from_position, jnp.concatenate(pair, axis=0)).reshape(32, 8, 128).astype(BF)
    tm_start(ts, tr, send_t, recv_t)
    tm_wait(ts, tr, send_t, recv_t)
    from_peer = one_hot_t(256, by_peer)
    for j in range(5):
        both = dot(from_peer, tr[:, j].reshape(256, 128)).astype(BF)
        for n in range(2):
            if 2 * j + n < LT:
                lanes = slice(128 * (2 * j + n), 128 * (2 * j + n) + 128)
                temporal_ref[:, :, lanes] = both[128 * n : 128 * n + 128].reshape(2, 64, 128)


def per_device(*args):
    whole = jax.ShapeDtypeStruct((2, 64, D), BF)
    dma = pltpu.SemaphoreType.DMA
    vmem = pltpu.VMEM
    return pl.pallas_call(
        kernel,
        out_shape=(whole, whole),
        in_specs=[pl.BlockSpec(memory_space=vmem)] * 6,
        out_specs=(pl.BlockSpec(memory_space=vmem),) * 2,
        scratch_shapes=[
            vmem((3, 144, 8, 128), BF),
            vmem((NS, 3, 9, 8, 128), BF),
            vmem((NS, 9, 8, 128), BF),
            vmem((NS, 9, 8, 128), BF),
            vmem((NT, LT, 8, 128), BF),
            vmem((NT, LT, 8, 128), BF),
            vmem((NT, 5, 8, 128), BF),
            vmem((NT, 5, 8, 128), BF),
            vmem((NT, 5, 8, 128), BF),
            vmem((NT, 5, 8, 128), BF),
            vmem((2, 80, 1024), BF),
            vmem((2, 1024, 128), BF),
            vmem((2, 80, 1024), BF),
            vmem((128, D), BF),
            vmem((128, D), BF),
            vmem((128, D), BF),
            vmem((128, D), F32),
            *[dma((NS,))] * 4,
            *[dma((NT,))] * 6,
            dma,
        ],
        compiler_params=pltpu.CompilerParams(
            collective_id=0, has_side_effects=True, vmem_limit_bytes=48 * 2**20
        ),
        cost_estimate=pl.CostEstimate(flops=2 * 10**9, bytes_accessed=3 * 10**6, transcendentals=3 * 10**6),
        name="attention",
    )(*args)


def solution(mesh):
    spec = P("tm", "space", None)
    return jax.shard_map(
        per_device, mesh=mesh, in_specs=(spec,) * 6, out_specs=(spec, spec), check_vma=False
    )
```

```python
import math

import jax
import jax.numpy as jnp
from jax import lax
from jax.experimental import pallas as pl
from jax.experimental.pallas import tpu as pltpu
from jax.sharding import PartitionSpec as P

D = 1152
HEADS = 16
HS = 72
LT = 9
NS = 16
NT = 32
BF = jnp.bfloat16
F32 = jnp.float32
MESH = pl.DeviceIdType.MESH
FACTOR = math.log2(math.e) / math.sqrt(HS)


def dot(a, b):
    return lax.dot_general(a, b, (((1,), (0,)), ((), ())), preferred_element_type=F32)


def dot_nt(a, b):
    return lax.dot_general(a, b, (((1,), (1,)), ((), ())), preferred_element_type=F32)


def one_hot(n, column_of_row):
    rows = lax.broadcasted_iota(jnp.int32, (n, n), 0)
    cols = lax.broadcasted_iota(jnp.int32, (n, n), 1)
    return jnp.where(cols == column_of_row(rows), 1.0, 0.0).astype(BF)


def one_hot_t(n, row_of_column):
    rows = lax.broadcasted_iota(jnp.int32, (n, n), 0)
    cols = lax.broadcasted_iota(jnp.int32, (n, n), 1)
    return jnp.where(rows == row_of_column(cols), 1.0, 0.0).astype(BF)


def others(body):
    lax.fori_loop(0, 14, body, 0)
    body(15, 0)


def bits(r, low, count):
    return (r >> low) & ((1 << count) - 1)


def frame_major(r):
    return bits(r, 6, 1) * 128 + bits(r, 7, 1) * 64 + bits(r, 0, 6)


def by_peer(r):
    return bits(r, 2, 1) * 128 + bits(r, 1, 1) * 64 + bits(r, 3, 5) * 2 + bits(r, 0, 1)


def by_position(r):
    return bits(r, 1, 5) * 8 + bits(r, 7, 1) * 4 + bits(r, 0, 1) * 2 + bits(r, 6, 1)


def kernel(
    q_hbm, k_hbm, v_hbm, stream_hbm, qt_hbm, kt_hbm, spatial_ref, temporal_ref,
    staged, xt, rs, osend, orecv, qks, qkr, vs, vr, ts, tr, q_f, k_f, v_f, q_p, k_p, v_p, o_p,
    send_x, recv_x, send_o, recv_o, send_qk, recv_qk, send_v, recv_v, send_t, recv_t, loads,
):
    s = lax.axis_index("space")
    t = lax.axis_index("tm")

    z, y, core = lax.div(t, 4), lax.rem(lax.div(t, 2), 2), lax.rem(t, 2)
    inputs = [
        pltpu.make_async_copy(ref, staged.at[n], loads.at[n])
        for n, ref in enumerate((q_hbm, k_hbm, v_hbm, qt_hbm, kt_hbm, stream_hbm))
    ]

    def other(i, side):
        k = 7 - lax.div(i, 2)
        step = lax.div(k + 1, 2) * (2 * lax.rem(k, 2) - 1)
        return 4 * lax.rem(z + (1 - 2 * core) * step + 8, 8) + 2 * side + lax.rem(core + i, 2)

    def far(i):
        return other(i, 1 - y)

    def near(i):
        return other(i, y)

    def line(i):
        m = 3 - i
        return 2 * lax.rem(lax.div(lax.rem(s, 4), 2) + lax.div(m, 2), 2) + lax.rem(s + m, 2)

    def ring(i):
        step = 2 - lax.div(i + 1, 2)
        return lax.rem(lax.div(s, 4) + step * (1 - 2 * lax.rem(i + core, 2)) + 4, 4)

    def across(i):
        return 4 * ring(lax.div(i, 4)) + line(lax.rem(i, 4))

    barrier = pltpu.get_barrier_semaphore()

    def greet(axis, peer):
        def body(i, c):
            pl.semaphore_signal(barrier, inc=1, device_id={axis: peer(i)}, device_id_type=MESH)
            return c

        return body

    lax.fori_loop(0, 16, greet("tm", far), 0)
    others(greet("tm", near))
    lax.fori_loop(0, NS - 1, greet("space", across), 0)
    for copy in inputs:
        copy.start()

    eye = one_hot(128, lambda r: r)

    for a in range(3):
        inputs[a].wait()
        for j in range(LT):
            block = staged[a, :, :, 128 * j : 128 * j + 128].reshape(128, 128)
            xt[a, 16 * j : 16 * j + 16] = dot_nt(eye, block).reshape(16, 8, 128).astype(BF)

    pl.semaphore_wait(barrier, NS + NT - 2)

    def space_x(p, at):
        return pltpu.make_async_remote_copy(
            src_ref=xt.at[:, pl.ds(9 * p, 9)], dst_ref=rs.at[at], send_sem=send_x.at[p], recv_sem=recv_x.at[at],
            device_id={"space": p}, device_id_type=MESH)

    def tm_copy(src, dst, send, recv, p, at, part=slice(None)):
        return pltpu.make_async_remote_copy(
            src_ref=src.at[p, part], dst_ref=dst.at[at, part], send_sem=send.at[p], recv_sem=recv.at[at],
            device_id={"tm": p}, device_id_type=MESH)

    def start_far(src, dst, send, recv, part=slice(None), low=0, high=16):
        def body(i, c):
            tm_copy(src, dst, send, recv, far(i), t, part).start()
            return c

        lax.fori_loop(low, high, body, 0)

    def start_near(src, dst, send, recv, part=slice(None)):
        def body(i, c):
            tm_copy(src, dst, send, recv, near(i), t, part).start()
            return c

        others(body)
        pltpu.make_async_copy(src.at[t, part], dst.at[t, part], recv.at[t]).start()

    def wait_tm(dst, recv, part=slice(None)):
        def body(p, c):
            pltpu.make_async_copy(dst.at[p, part], dst.at[p, part], recv.at[p]).wait()
            return c

        lax.fori_loop(0, NT, body, 0)

    def sent_tm(src, send, part=slice(None)):
        def body(i, c):
            p = lax.rem(t + i, NT)
            tm_copy(src, src, send, send, p, p, part).wait_send()
            return c

        lax.fori_loop(1, NT, body, 0)

    def start_x(i, c):
        space_x(across(i), s).start()
        return c

    lax.fori_loop(0, NS - 1, start_x, 0)
    pltpu.make_async_copy(xt.at[:, pl.ds(9 * s, 9)], rs.at[s], recv_x.at[s]).start()

    to_peer = one_hot(256, by_peer)
    inputs[3].wait()
    inputs[4].wait()
    for j in range(LT):
        pair = jnp.concatenate(
            [staged[n, :, :, 128 * j : 128 * j + 128].reshape(128, 128) for n in (3, 4)], axis=0
        )
        qks[:, j] = dot(to_peer, pair).reshape(32, 8, 128).astype(BF)
    start_near(qks, qkr, send_qk, recv_qk)

    def sent_x(i, c):
        p = lax.rem(s + i, NS)
        space_x(p, p).wait_send()
        return c

    lax.fori_loop(1, NS, sent_x, 0)
    start_far(qks, qkr, send_qk, recv_qk, high=8)

    sort = one_hot_t(256, frame_major)
    sort_t = one_hot(256, frame_major)

    def arrange(i, c):
        pair = lax.rem(lax.div(s, 2) + i, NS // 2)
        for m in range(2):
            p = 2 * pair + m
            pltpu.make_async_copy(rs.at[p], rs.at[p], recv_x.at[p]).wait()
        both = jnp.concatenate([rs[2 * pair + m].reshape(216, 128) for m in range(2)], axis=1)
        qv = dot(both, sort)
        keys = dot_nt(sort_t, both[HS : 2 * HS])
        at = pl.ds(pl.multiple_of(pair * 128, 128), 128)
        for f in range(2):
            q_f[f, :HS, at] = qv[:HS, 128 * f : 128 * f + 128].astype(BF)
            v_f[f, :HS, at] = qv[2 * HS :, 128 * f : 128 * f + 128].astype(BF)
            k_f[f, at, :HS] = keys[128 * f : 128 * f + 128].astype(BF)
        return c

    lax.fori_loop(0, NS // 2, arrange, 0)

    def copy_o(p, at):
        return pltpu.make_async_remote_copy(
            src_ref=osend.at[p], dst_ref=orecv.at[at], send_sem=send_o.at[p], recv_sem=recv_o.at[at],
            device_id={"space": p}, device_id_type=MESH)

    own_o = pltpu.make_async_copy(osend.at[s], orecv.at[s], recv_o.at[s])

    def attend(i, c):
        tile = ring(i)
        at = pl.ds(pl.multiple_of(tile * 256, 256), 256)
        mixed = []
        for f in range(2):
            scores = dot(k_f[f, :, :HS], q_f[f, :HS, at])
            top = jnp.max(scores, axis=0, keepdims=True) * FACTOR
            raised = jnp.exp2(scores * FACTOR - top)
            total = jnp.sum(raised, axis=0, keepdims=True)
            mix = dot(v_f[f, :HS, :], raised.astype(BF))
            mixed.append((mix / total).astype(BF))
        for m in range(2):
            back = dot(jnp.concatenate([x[:, 128 * m : 128 * m + 128] for x in mixed], axis=1), sort_t)
            for n in range(2):
                osend[4 * tile + 2 * m + n] = back[:, 128 * n : 128 * n + 128].reshape(9, 8, 128).astype(BF)
        for n in range(4):
            p = 4 * tile + line(n)

            @pl.when(p != s)
            def _():
                copy_o(p, s).start()

            @pl.when(p == s)
            def _():
                own_o.start()

        return c

    lax.fori_loop(0, 4, attend, 0)
    inputs[5].wait()

    def wait_o(p, c):
        pltpu.make_async_copy(orecv.at[p], orecv.at[p], recv_o.at[p]).wait()
        return c

    zeros = jnp.zeros((128, 128), BF)

    def pack_v(j):
        pair = []
        for n in (2 * j, 2 * j + 1):
            if n == LT:
                pair.append(zeros)
                continue
            rows = [orecv[r // 9, r % 9] for r in range(16 * n, 16 * n + 16)]
            block = dot_nt(eye, jnp.concatenate(rows, axis=0)).astype(BF)
            lanes = slice(128 * n, 128 * n + 128)
            spatial_ref[:, :, lanes] = block.reshape(2, 64, 128)
            stream = staged[5, :, :, lanes].reshape(128, 128)
            pair.append((stream.astype(F32) + block.astype(F32)).astype(BF))
        vs[:, j] = dot(to_peer, jnp.concatenate(pair, axis=0)).reshape(32, 8, 128).astype(BF)

    def unpack_v(j):
        both = dot(to_position, vr[:, j].reshape(256, 128)).astype(BF)
        for n in range(2):
            if 2 * j + n < LT:
                v_p[:, 128 * (2 * j + n) : 128 * (2 * j + n) + 128] = both[128 * n : 128 * n + 128]

    first_v, last_v = slice(0, 3), slice(3, 5)
    lax.fori_loop(0, 11, wait_o, 0)
    start_far(qks, qkr, send_qk, recv_qk, low=8)
    for j in range(3):
        pack_v(j)
    start_far(vs, vr, send_v.at[0], recv_v.at[0], first_v)
    start_near(vs, vr, send_v.at[0], recv_v.at[0], first_v)
    lax.fori_loop(11, NS, wait_o, 0)
    for j in range(3, 5):
        pack_v(j)
    start_far(vs, vr, send_v.at[1], recv_v.at[1], last_v)
    start_near(vs, vr, send_v.at[1], recv_v.at[1], last_v)

    to_position = one_hot(256, by_position)
    wait_tm(qkr, recv_qk)
    for j in range(LT):
        both = dot(to_position, qkr[:, j].reshape(256, 128)).astype(BF)
        q_p[:, 128 * j : 128 * j + 128] = both[:128]
        k_p[:, 128 * j : 128 * j + 128] = both[128:]

    rows = lax.broadcasted_iota(jnp.int32, (128, 128), 0)
    cols = lax.broadcasted_iota(jnp.int32, (128, 128), 1)
    same = (rows >> 6) == (cols >> 6)

    def head(h):
        low, high = HS * h // 128 * 128, -(-HS * (h + 1) // 128) * 128
        lane = lax.broadcasted_iota(jnp.int32, (128, high - low), 1) + low
        mine = (lane >= HS * h) & (lane < HS * (h + 1))
        keys = jnp.where(mine, k_p[:, low:high].astype(F32), 0.0).astype(BF)
        scores = jnp.where(same, dot_nt(q_p[:, low:high], keys), -jnp.inf)
        top = jnp.max(scores, axis=1, keepdims=True) * FACTOR
        raised = jnp.exp2(scores * FACTOR - top)
        total = jnp.sum(raised, axis=1, keepdims=True)
        mix = dot(raised.astype(BF), v_p[:, low:high]) / total
        o_p[:, low:high] = jnp.where(mine, mix, o_p[:, low:high])

    from_position = one_hot_t(256, by_position)

    def pack_t(j):
        pair = [o_p[:, 128 * n : 128 * n + 128].astype(BF) if n < LT else zeros for n in (2 * j, 2 * j + 1)]
        ts[:, j] = dot(from_position, jnp.concatenate(pair, axis=0)).reshape(32, 8, 128).astype(BF)

    first_t, last_t = slice(0, 2), slice(2, 5)
    wait_tm(vr, recv_v.at[0], first_v)
    for j in range(3):
        unpack_v(j)
    for h in range(8):
        head(h)
    for j in range(2):
        pack_t(j)
    start_far(ts, tr, send_t.at[0], recv_t.at[0], first_t)
    start_near(ts, tr, send_t.at[0], recv_t.at[0], first_t)
    for h in range(8, 10):
        head(h)
    wait_tm(vr, recv_v.at[1], last_v)
    for j in range(3, 5):
        unpack_v(j)
    for h in range(10, HEADS):
        head(h)
    for j in range(2, 5):
        pack_t(j)
    start_far(ts, tr, send_t.at[1], recv_t.at[1], last_t)
    start_near(ts, tr, send_t.at[1], recv_t.at[1], last_t)

    from_peer = one_hot_t(256, by_peer)

    def unpack_t(j):
        both = dot(from_peer, tr[:, j].reshape(256, 128)).astype(BF)
        for n in range(2):
            if 2 * j + n < LT:
                lanes = slice(128 * (2 * j + n), 128 * (2 * j + n) + 128)
                temporal_ref[:, :, lanes] = both[128 * n : 128 * n + 128].reshape(2, 64, 128)

    wait_tm(tr, recv_t.at[0], first_t)
    for j in range(2):
        unpack_t(j)
    wait_tm(tr, recv_t.at[1], last_t)
    for j in range(2, 5):
        unpack_t(j)

    def sent_o(i, c):
        p = lax.rem(s + i, NS)
        copy_o(p, p).wait_send()
        return c

    lax.fori_loop(1, NS, sent_o, 0)
    sent_tm(qks, send_qk)
    for n, part in enumerate((first_v, last_v)):
        sent_tm(vs, send_v.at[n], part)
    for n, part in enumerate((first_t, last_t)):
        sent_tm(ts, send_t.at[n], part)


def per_device(*args):
    whole = jax.ShapeDtypeStruct((2, 64, D), BF)
    dma = pltpu.SemaphoreType.DMA
    vmem = pltpu.VMEM
    return pl.pallas_call(
        kernel,
        out_shape=(whole, whole),
        in_specs=[pl.BlockSpec(memory_space=pltpu.HBM)] * 6,
        out_specs=(pl.BlockSpec(memory_space=vmem),) * 2,
        scratch_shapes=[
            vmem((6, 2, 64, D), BF),
            vmem((3, 144, 8, 128), BF),
            vmem((NS, 3, 9, 8, 128), BF),
            vmem((NS, 9, 8, 128), BF),
            vmem((NS, 9, 8, 128), BF),
            vmem((NT, LT, 8, 128), BF),
            vmem((NT, LT, 8, 128), BF),
            vmem((NT, 5, 8, 128), BF),
            vmem((NT, 5, 8, 128), BF),
            vmem((NT, 5, 8, 128), BF),
            vmem((NT, 5, 8, 128), BF),
            vmem((2, 80, 1024), BF),
            vmem((2, 1024, 128), BF),
            vmem((2, 80, 1024), BF),
            vmem((128, D), BF),
            vmem((128, D), BF),
            vmem((128, D), BF),
            vmem((128, D), F32),
            *[dma((NS,))] * 4,
            *[dma((NT,))] * 2,
            *[dma((2, NT))] * 4,
            dma((6,)),
        ],
        compiler_params=pltpu.CompilerParams(
            collective_id=0, has_side_effects=True, vmem_limit_bytes=60 * 2**20
        ),
        cost_estimate=pl.CostEstimate(flops=2 * 10**9, bytes_accessed=3 * 10**6, transcendentals=3 * 10**6),
        name="attention",
    )(*args)


def solution(mesh):
    spec = P("tm", "space", None)
    return jax.shard_map(
        per_device, mesh=mesh, in_specs=(spec,) * 6, out_specs=(spec, spec), check_vma=False
    )
```

```python
import math

import jax
import jax.numpy as jnp
from jax import lax
from jax.experimental import pallas as pl
from jax.experimental.pallas import tpu as pltpu
from jax.sharding import PartitionSpec as P

D = 1152
HEADS = 16
HS = 72
LT = 9
NS = 16
NT = 32
BF = jnp.bfloat16
F32 = jnp.float32
MESH = pl.DeviceIdType.MESH
FACTOR = math.log2(math.e) / math.sqrt(HS)


def dot(a, b):
    return lax.dot_general(a, b, (((1,), (0,)), ((), ())), preferred_element_type=F32)


def dot_nt(a, b):
    return lax.dot_general(a, b, (((1,), (1,)), ((), ())), preferred_element_type=F32)


def one_hot(n, column_of_row):
    rows = lax.broadcasted_iota(jnp.int32, (n, n), 0)
    cols = lax.broadcasted_iota(jnp.int32, (n, n), 1)
    return jnp.where(cols == column_of_row(rows), 1.0, 0.0).astype(BF)


def one_hot_t(n, row_of_column):
    rows = lax.broadcasted_iota(jnp.int32, (n, n), 0)
    cols = lax.broadcasted_iota(jnp.int32, (n, n), 1)
    return jnp.where(rows == row_of_column(cols), 1.0, 0.0).astype(BF)


def others(body):
    lax.fori_loop(0, 14, body, 0)
    body(15, 0)


def bits(r, low, count):
    return (r >> low) & ((1 << count) - 1)


def frame_major(r):
    return bits(r, 6, 1) * 128 + bits(r, 7, 1) * 64 + bits(r, 0, 6)


def by_peer(r):
    return bits(r, 2, 1) * 128 + bits(r, 1, 1) * 64 + bits(r, 3, 5) * 2 + bits(r, 0, 1)


def by_position(r):
    return bits(r, 1, 5) * 8 + bits(r, 7, 1) * 4 + bits(r, 0, 1) * 2 + bits(r, 6, 1)


def kernel(
    q_hbm, k_hbm, v_hbm, stream_hbm, qt_hbm, kt_hbm, spatial_hbm, temporal_hbm,
    spatial_ref, temporal_ref, staged, xt, rs, osend, orecv, qks, qkr, vs, vr, ts, tr, q_f, k_f, v_f, q_p, k_p, v_p, o_p,
    send_x, recv_x, send_o, recv_o, send_qk, recv_qk, send_v, recv_v, send_t, recv_t, loads, stores,
):
    s = lax.axis_index("space")
    t = lax.axis_index("tm")

    z, y, core = lax.div(t, 4), lax.rem(lax.div(t, 2), 2), lax.rem(t, 2)
    inputs = [
        pltpu.make_async_copy(ref, staged.at[n], loads.at[n])
        for n, ref in enumerate((q_hbm, k_hbm, v_hbm, qt_hbm, kt_hbm, stream_hbm))
    ]

    def other(i, side):
        k = 7 - lax.div(i, 2)
        step = lax.div(k + 1, 2) * (2 * lax.rem(k, 2) - 1)
        return 4 * lax.rem(z + (1 - 2 * core) * step + 8, 8) + 2 * side + lax.rem(core + i, 2)

    def far(i):
        return other(i, 1 - y)

    def near(i):
        return other(i, y)

    def line(i):
        m = 3 - i
        return 2 * lax.rem(lax.div(lax.rem(s, 4), 2) + lax.div(m, 2), 2) + lax.rem(s + m, 2)

    def ring(i):
        step = 2 - lax.div(i + 1, 2)
        return lax.rem(lax.div(s, 4) + step * (1 - 2 * lax.rem(i + core, 2)) + 4, 4)

    def across(i):
        return 4 * ring(lax.div(i, 4)) + line(lax.rem(i, 4))

    barrier = pltpu.get_barrier_semaphore()

    def greet(axis, peer):
        def body(i, c):
            pl.semaphore_signal(barrier, inc=1, device_id={axis: peer(i)}, device_id_type=MESH)
            return c

        return body

    lax.fori_loop(0, 16, greet("tm", far), 0)
    others(greet("tm", near))
    lax.fori_loop(0, NS - 1, greet("space", across), 0)
    for copy in inputs:
        copy.start()

    eye = one_hot(128, lambda r: r)

    for a in range(3):
        inputs[a].wait()
        for j in range(LT):
            block = staged[a, :, :, 128 * j : 128 * j + 128].reshape(128, 128)
            xt[a, 16 * j : 16 * j + 16] = dot_nt(eye, block).reshape(16, 8, 128).astype(BF)

    pl.semaphore_wait(barrier, NS + NT - 2)

    def space_x(p, at):
        return pltpu.make_async_remote_copy(
            src_ref=xt.at[:, pl.ds(9 * p, 9)], dst_ref=rs.at[at], send_sem=send_x.at[p], recv_sem=recv_x.at[at],
            device_id={"space": p}, device_id_type=MESH)

    def tm_copy(src, dst, send, recv, p, at, part=slice(None)):
        return pltpu.make_async_remote_copy(
            src_ref=src.at[p, part], dst_ref=dst.at[at, part], send_sem=send.at[p], recv_sem=recv.at[at],
            device_id={"tm": p}, device_id_type=MESH)

    def start_far(src, dst, send, recv, part=slice(None), low=0, high=16):
        def body(i, c):
            tm_copy(src, dst, send, recv, far(i), t, part).start()
            return c

        lax.fori_loop(low, high, body, 0)

    def start_near(src, dst, send, recv, part=slice(None)):
        def body(i, c):
            tm_copy(src, dst, send, recv, near(i), t, part).start()
            return c

        others(body)
        pltpu.make_async_copy(src.at[t, part], dst.at[t, part], recv.at[t]).start()

    def wait_tm(dst, recv, part=slice(None)):
        def body(p, c):
            pltpu.make_async_copy(dst.at[p, part], dst.at[p, part], recv.at[p]).wait()
            return c

        lax.fori_loop(0, NT, body, 0)

    def sent_tm(src, send, part=slice(None)):
        def body(i, c):
            p = lax.rem(t + i, NT)
            tm_copy(src, src, send, send, p, p, part).wait_send()
            return c

        lax.fori_loop(1, NT, body, 0)

    def start_x(i, c):
        space_x(across(i), s).start()
        return c

    lax.fori_loop(0, NS - 1, start_x, 0)
    pltpu.make_async_copy(xt.at[:, pl.ds(9 * s, 9)], rs.at[s], recv_x.at[s]).start()

    to_peer = one_hot(256, by_peer)
    inputs[3].wait()
    inputs[4].wait()
    for j in range(LT):
        pair = jnp.concatenate(
            [staged[n, :, :, 128 * j : 128 * j + 128].reshape(128, 128) for n in (3, 4)], axis=0
        )
        qks[:, j] = dot(to_peer, pair).reshape(32, 8, 128).astype(BF)
    start_near(qks, qkr, send_qk, recv_qk)

    def sent_x(i, c):
        p = lax.rem(s + i, NS)
        space_x(p, p).wait_send()
        return c

    lax.fori_loop(1, NS, sent_x, 0)
    start_far(qks, qkr, send_qk, recv_qk, high=8)

    sort = one_hot_t(256, frame_major)
    sort_t = one_hot(256, frame_major)

    def arrange(i, c):
        pair = lax.rem(lax.div(s, 2) + i, NS // 2)
        for m in range(2):
            p = 2 * pair + m
            pltpu.make_async_copy(rs.at[p], rs.at[p], recv_x.at[p]).wait()
        both = jnp.concatenate([rs[2 * pair + m].reshape(216, 128) for m in range(2)], axis=1)
        qv = dot(both, sort)
        keys = dot_nt(sort_t, both[HS : 2 * HS])
        at = pl.ds(pl.multiple_of(pair * 128, 128), 128)
        for f in range(2):
            q_f[f, :HS, at] = qv[:HS, 128 * f : 128 * f + 128].astype(BF)
            v_f[f, :HS, at] = qv[2 * HS :, 128 * f : 128 * f + 128].astype(BF)
            k_f[f, at, :HS] = keys[128 * f : 128 * f + 128].astype(BF)
        return c

    lax.fori_loop(0, NS // 2, arrange, 0)

    def copy_o(p, at):
        return pltpu.make_async_remote_copy(
            src_ref=osend.at[p], dst_ref=orecv.at[at], send_sem=send_o.at[p], recv_sem=recv_o.at[at],
            device_id={"space": p}, device_id_type=MESH)

    own_o = pltpu.make_async_copy(osend.at[s], orecv.at[s], recv_o.at[s])

    def attend(i, c):
        tile = ring(i)
        at = pl.ds(pl.multiple_of(tile * 256, 256), 256)
        mixed = []
        for f in range(2):
            scores = dot(k_f[f, :, :HS], q_f[f, :HS, at])
            top = jnp.max(scores, axis=0, keepdims=True) * FACTOR
            raised = jnp.exp2(scores * FACTOR - top)
            total = jnp.sum(raised, axis=0, keepdims=True)
            mix = dot(v_f[f, :HS, :], raised.astype(BF))
            mixed.append((mix / total).astype(BF))
        for m in range(2):
            back = dot(jnp.concatenate([x[:, 128 * m : 128 * m + 128] for x in mixed], axis=1), sort_t)
            for n in range(2):
                osend[4 * tile + 2 * m + n] = back[:, 128 * n : 128 * n + 128].reshape(9, 8, 128).astype(BF)
        for n in range(4):
            p = 4 * tile + line(n)

            @pl.when(p != s)
            def _():
                copy_o(p, s).start()

            @pl.when(p == s)
            def _():
                own_o.start()

        return c

    lax.fori_loop(0, 4, attend, 0)
    inputs[5].wait()

    def wait_o(p, c):
        pltpu.make_async_copy(orecv.at[p], orecv.at[p], recv_o.at[p]).wait()
        return c

    zeros = jnp.zeros((128, 128), BF)

    def pack_v(j):
        pair = []
        for n in (2 * j, 2 * j + 1):
            if n == LT:
                pair.append(zeros)
                continue
            rows = [orecv[r // 9, r % 9] for r in range(16 * n, 16 * n + 16)]
            block = dot_nt(eye, jnp.concatenate(rows, axis=0)).astype(BF)
            lanes = slice(128 * n, 128 * n + 128)
            spatial_ref[:, :, lanes] = block.reshape(2, 64, 128)
            stream = staged[5, :, :, lanes].reshape(128, 128)
            pair.append((stream.astype(F32) + block.astype(F32)).astype(BF))
        vs[:, j] = dot(to_peer, jnp.concatenate(pair, axis=0)).reshape(32, 8, 128).astype(BF)

    def unpack_v(j):
        both = dot(to_position, vr[:, j].reshape(256, 128)).astype(BF)
        for n in range(2):
            if 2 * j + n < LT:
                v_p[:, 128 * (2 * j + n) : 128 * (2 * j + n) + 128] = both[128 * n : 128 * n + 128]

    first_v, last_v = slice(0, 3), slice(3, 5)
    lax.fori_loop(0, 11, wait_o, 0)
    start_far(qks, qkr, send_qk, recv_qk, low=8)
    for j in range(3):
        pack_v(j)
    start_far(vs, vr, send_v.at[0], recv_v.at[0], first_v)
    start_near(vs, vr, send_v.at[0], recv_v.at[0], first_v)
    lax.fori_loop(11, NS, wait_o, 0)
    for j in range(3, 5):
        pack_v(j)
    start_far(vs, vr, send_v.at[1], recv_v.at[1], last_v)
    start_near(vs, vr, send_v.at[1], recv_v.at[1], last_v)

    store_s = pltpu.make_async_copy(spatial_ref, spatial_hbm, stores.at[0])
    store_s.start()

    to_position = one_hot(256, by_position)
    wait_tm(qkr, recv_qk)
    for j in range(LT):
        both = dot(to_position, qkr[:, j].reshape(256, 128)).astype(BF)
        q_p[:, 128 * j : 128 * j + 128] = both[:128]
        k_p[:, 128 * j : 128 * j + 128] = both[128:]

    rows = lax.broadcasted_iota(jnp.int32, (128, 128), 0)
    cols = lax.broadcasted_iota(jnp.int32, (128, 128), 1)
    same = (rows >> 6) == (cols >> 6)

    def head(h):
        low, high = HS * h // 128 * 128, -(-HS * (h + 1) // 128) * 128
        lane = lax.broadcasted_iota(jnp.int32, (128, high - low), 1) + low
        mine = (lane >= HS * h) & (lane < HS * (h + 1))
        keys = jnp.where(mine, k_p[:, low:high].astype(F32), 0.0).astype(BF)
        scores = jnp.where(same, dot_nt(q_p[:, low:high], keys), -jnp.inf)
        top = jnp.max(scores, axis=1, keepdims=True) * FACTOR
        raised = jnp.exp2(scores * FACTOR - top)
        total = jnp.sum(raised, axis=1, keepdims=True)
        mix = dot(raised.astype(BF), v_p[:, low:high]) / total
        o_p[:, low:high] = jnp.where(mine, mix, o_p[:, low:high])

    from_position = one_hot_t(256, by_position)

    def pack_t(j):
        pair = [o_p[:, 128 * n : 128 * n + 128].astype(BF) if n < LT else zeros for n in (2 * j, 2 * j + 1)]
        ts[:, j] = dot(from_position, jnp.concatenate(pair, axis=0)).reshape(32, 8, 128).astype(BF)

    first_t, last_t = slice(0, 2), slice(2, 5)
    wait_tm(vr, recv_v.at[0], first_v)
    for j in range(3):
        unpack_v(j)
    for h in range(8):
        head(h)
    for j in range(2):
        pack_t(j)
    start_far(ts, tr, send_t.at[0], recv_t.at[0], first_t)
    start_near(ts, tr, send_t.at[0], recv_t.at[0], first_t)
    for h in range(8, 10):
        head(h)
    wait_tm(vr, recv_v.at[1], last_v)
    for j in range(3, 5):
        unpack_v(j)
    for h in range(10, HEADS):
        head(h)
    for j in range(2, 5):
        pack_t(j)
    start_far(ts, tr, send_t.at[1], recv_t.at[1], last_t)
    start_near(ts, tr, send_t.at[1], recv_t.at[1], last_t)

    from_peer = one_hot_t(256, by_peer)

    def unpack_t(j):
        both = dot(from_peer, tr[:, j].reshape(256, 128)).astype(BF)
        for n in range(2):
            if 2 * j + n < LT:
                lanes = slice(128 * (2 * j + n), 128 * (2 * j + n) + 128)
                temporal_ref[:, :, lanes] = both[128 * n : 128 * n + 128].reshape(2, 64, 128)

    wait_tm(tr, recv_t.at[0], first_t)
    for j in range(2):
        unpack_t(j)
    store_a = pltpu.make_async_copy(
        temporal_ref.at[:, :, :512], temporal_hbm.at[:, :, :512], stores.at[1]
    )
    store_a.start()
    wait_tm(tr, recv_t.at[1], last_t)
    for j in range(2, 5):
        unpack_t(j)

    store_b = pltpu.make_async_copy(
        temporal_ref.at[:, :, 512:], temporal_hbm.at[:, :, 512:], stores.at[2]
    )
    store_b.start()

    def sent_o(i, c):
        p = lax.rem(s + i, NS)
        copy_o(p, p).wait_send()
        return c

    lax.fori_loop(1, NS, sent_o, 0)
    sent_tm(qks, send_qk)
    for n, part in enumerate((first_v, last_v)):
        sent_tm(vs, send_v.at[n], part)
    for n, part in enumerate((first_t, last_t)):
        sent_tm(ts, send_t.at[n], part)
    for copy in (store_s, store_a, store_b):
        copy.wait()


def per_device(*args):
    whole = jax.ShapeDtypeStruct((2, 64, D), BF)
    dma = pltpu.SemaphoreType.DMA
    vmem = pltpu.VMEM
    return pl.pallas_call(
        kernel,
        out_shape=(whole, whole),
        in_specs=[pl.BlockSpec(memory_space=pltpu.HBM)] * 6,
        out_specs=(pl.BlockSpec(memory_space=pltpu.HBM),) * 2,
        scratch_shapes=[
            vmem((2, 64, D), BF),
            vmem((2, 64, D), BF),
            vmem((6, 2, 64, D), BF),
            vmem((3, 144, 8, 128), BF),
            vmem((NS, 3, 9, 8, 128), BF),
            vmem((NS, 9, 8, 128), BF),
            vmem((NS, 9, 8, 128), BF),
            vmem((NT, LT, 8, 128), BF),
            vmem((NT, LT, 8, 128), BF),
            vmem((NT, 5, 8, 128), BF),
            vmem((NT, 5, 8, 128), BF),
            vmem((NT, 5, 8, 128), BF),
            vmem((NT, 5, 8, 128), BF),
            vmem((2, 80, 1024), BF),
            vmem((2, 1024, 128), BF),
            vmem((2, 80, 1024), BF),
            vmem((128, D), BF),
            vmem((128, D), BF),
            vmem((128, D), BF),
            vmem((128, D), F32),
            *[dma((NS,))] * 4,
            *[dma((NT,))] * 2,
            *[dma((2, NT))] * 4,
            dma((6,)),
            dma((3,)),
        ],
        compiler_params=pltpu.CompilerParams(
            collective_id=0, has_side_effects=True, vmem_limit_bytes=60 * 2**20
        ),
        cost_estimate=pl.CostEstimate(flops=2 * 10**9, bytes_accessed=3 * 10**6, transcendentals=3 * 10**6),
        name="attention",
    )(*args)


def solution(mesh):
    spec = P("tm", "space", None)
    return jax.shard_map(
        per_device, mesh=mesh, in_specs=(spec,) * 6, out_specs=(spec, spec), check_vma=False
    )
```

```python
import math

import jax
import jax.numpy as jnp
from jax import lax
from jax.experimental import pallas as pl
from jax.experimental.pallas import tpu as pltpu
from jax.sharding import PartitionSpec as P

D = 1152
HEADS = 16
HS = 72
LT = 9
NS = 16
NT = 32
BF = jnp.bfloat16
F32 = jnp.float32
MESH = pl.DeviceIdType.MESH
FACTOR = math.log2(math.e) / math.sqrt(HS)


def dot(a, b):
    return lax.dot_general(a, b, (((1,), (0,)), ((), ())), preferred_element_type=F32)


def dot_nt(a, b):
    return lax.dot_general(a, b, (((1,), (1,)), ((), ())), preferred_element_type=F32)


def one_hot(n, column_of_row):
    rows = lax.broadcasted_iota(jnp.int32, (n, n), 0)
    cols = lax.broadcasted_iota(jnp.int32, (n, n), 1)
    return jnp.where(cols == column_of_row(rows), 1.0, 0.0).astype(BF)


def one_hot_t(n, row_of_column):
    rows = lax.broadcasted_iota(jnp.int32, (n, n), 0)
    cols = lax.broadcasted_iota(jnp.int32, (n, n), 1)
    return jnp.where(rows == row_of_column(cols), 1.0, 0.0).astype(BF)


def others(body):
    lax.fori_loop(0, 14, body, 0)
    body(15, 0)


def bits(r, low, count):
    return (r >> low) & ((1 << count) - 1)


def frame_major(r):
    return bits(r, 6, 1) * 128 + bits(r, 7, 1) * 64 + bits(r, 0, 6)


def by_peer(r):
    return bits(r, 2, 1) * 128 + bits(r, 1, 1) * 64 + bits(r, 3, 5) * 2 + bits(r, 0, 1)


def by_position(r):
    return bits(r, 1, 5) * 8 + bits(r, 7, 1) * 4 + bits(r, 0, 1) * 2 + bits(r, 6, 1)


def kernel(
    q_hbm, k_hbm, v_hbm, stream_hbm, qt_hbm, kt_hbm, spatial_hbm, temporal_hbm,
    spatial_ref, temporal_ref, staged, xt, rs, osend, orecv, qks, qkr, vs, vr, ts, tr, q_f, k_f, v_f, q_p, k_p, v_p, o_p,
    send_x, recv_x, send_o, recv_o, send_qk, recv_qk, send_v, recv_v, send_t, recv_t, loads, stores,
):
    s = lax.axis_index("space")
    t = lax.axis_index("tm")

    z, y, core = lax.div(t, 4), lax.rem(lax.div(t, 2), 2), lax.rem(t, 2)
    inputs = [
        pltpu.make_async_copy(ref, staged.at[n], loads.at[n])
        for n, ref in enumerate((q_hbm, k_hbm, v_hbm, qt_hbm, kt_hbm, stream_hbm))
    ]

    def other(i, side):
        k = 7 - lax.div(i, 2)
        step = lax.div(k + 1, 2) * (2 * lax.rem(k, 2) - 1)
        return 4 * lax.rem(z + (1 - 2 * core) * step + 8, 8) + 2 * side + lax.rem(core + i, 2)

    def far(i):
        return other(i, 1 - y)

    def near(i):
        return other(i, y)

    def line(i):
        m = 3 - i
        return 2 * lax.rem(lax.div(lax.rem(s, 4), 2) + lax.div(m, 2), 2) + lax.rem(s + m, 2)

    def ring(i):
        step = 2 - lax.div(i + 1, 2)
        return lax.rem(lax.div(s, 4) + step * (1 - 2 * lax.rem(i + core, 2)) + 4, 4)

    def across(i):
        return 4 * ring(lax.div(i, 4)) + line(lax.rem(i, 4))

    barrier = pltpu.get_barrier_semaphore()

    def greet(axis, peer):
        def body(i, c):
            pl.semaphore_signal(barrier, inc=1, device_id={axis: peer(i)}, device_id_type=MESH)
            return c

        return body

    lax.fori_loop(0, 16, greet("tm", far), 0)
    others(greet("tm", near))
    lax.fori_loop(0, NS - 1, greet("space", across), 0)
    for copy in inputs:
        copy.start()

    eye = one_hot(128, lambda r: r)

    for a in range(3):
        inputs[a].wait()
        for j in range(LT):
            block = staged[a, :, :, 128 * j : 128 * j + 128].reshape(128, 128)
            xt[a, 16 * j : 16 * j + 16] = dot_nt(eye, block).reshape(16, 8, 128).astype(BF)

    pl.semaphore_wait(barrier, NS + NT - 2)

    def space_x(p, at):
        return pltpu.make_async_remote_copy(
            src_ref=xt.at[:, pl.ds(9 * p, 9)], dst_ref=rs.at[at], send_sem=send_x.at[p], recv_sem=recv_x.at[at],
            device_id={"space": p}, device_id_type=MESH)

    def tm_copy(src, dst, send, recv, p, at, part=slice(None)):
        return pltpu.make_async_remote_copy(
            src_ref=src.at[p, part], dst_ref=dst.at[at, part], send_sem=send.at[p], recv_sem=recv.at[at],
            device_id={"tm": p}, device_id_type=MESH)

    def start_far(src, dst, send, recv, part=slice(None), low=0, high=16):
        def body(i, c):
            tm_copy(src, dst, send, recv, far(i), t, part).start()
            return c

        lax.fori_loop(low, high, body, 0)

    def start_near(src, dst, send, recv, part=slice(None)):
        def body(i, c):
            tm_copy(src, dst, send, recv, near(i), t, part).start()
            return c

        others(body)
        pltpu.make_async_copy(src.at[t, part], dst.at[t, part], recv.at[t]).start()

    def start_all(src, dst, send, recv, part):
        def body(i, c):
            tm_copy(src, dst, send, recv, far(i), t, part).start()
            tm_copy(src, dst, send, recv, near(i), t, part).start()
            return c

        others(body)
        tm_copy(src, dst, send, recv, far(14), t, part).start()
        pltpu.make_async_copy(src.at[t, part], dst.at[t, part], recv.at[t]).start()

    def wait_tm(dst, recv, part=slice(None)):
        def body(p, c):
            pltpu.make_async_copy(dst.at[p, part], dst.at[p, part], recv.at[p]).wait()
            return c

        lax.fori_loop(0, NT, body, 0)

    def sent_tm(src, send, part=slice(None)):
        def body(i, c):
            p = lax.rem(t + i, NT)
            tm_copy(src, src, send, send, p, p, part).wait_send()
            return c

        lax.fori_loop(1, NT, body, 0)

    def start_x(i, c):
        space_x(across(i), s).start()
        return c

    lax.fori_loop(0, NS - 1, start_x, 0)
    pltpu.make_async_copy(xt.at[:, pl.ds(9 * s, 9)], rs.at[s], recv_x.at[s]).start()

    to_peer = one_hot(256, by_peer)
    inputs[3].wait()
    inputs[4].wait()
    for j in range(LT):
        pair = jnp.concatenate(
            [staged[n, :, :, 128 * j : 128 * j + 128].reshape(128, 128) for n in (3, 4)], axis=0
        )
        qks[:, j] = dot(to_peer, pair).reshape(32, 8, 128).astype(BF)
    start_near(qks, qkr, send_qk, recv_qk)

    def sent_x(i, c):
        p = lax.rem(s + i, NS)
        space_x(p, p).wait_send()
        return c

    lax.fori_loop(1, NS, sent_x, 0)
    start_far(qks, qkr, send_qk, recv_qk, high=8)

    sort = one_hot_t(256, frame_major)
    sort_t = one_hot(256, frame_major)

    def arrange(i, c):
        pair = lax.rem(lax.div(s, 2) + i, NS // 2)
        for m in range(2):
            p = 2 * pair + m
            pltpu.make_async_copy(rs.at[p], rs.at[p], recv_x.at[p]).wait()
        both = jnp.concatenate([rs[2 * pair + m].reshape(216, 128) for m in range(2)], axis=1)
        qv = dot(both, sort)
        keys = dot_nt(sort_t, both[HS : 2 * HS])
        at = pl.ds(pl.multiple_of(pair * 128, 128), 128)
        for f in range(2):
            q_f[f, :HS, at] = qv[:HS, 128 * f : 128 * f + 128].astype(BF)
            v_f[f, :HS, at] = qv[2 * HS :, 128 * f : 128 * f + 128].astype(BF)
            k_f[f, at, :HS] = keys[128 * f : 128 * f + 128].astype(BF)
        return c

    lax.fori_loop(0, NS // 2, arrange, 0)

    def copy_o(p, at):
        return pltpu.make_async_remote_copy(
            src_ref=osend.at[p], dst_ref=orecv.at[at], send_sem=send_o.at[p], recv_sem=recv_o.at[at],
            device_id={"space": p}, device_id_type=MESH)

    own_o = pltpu.make_async_copy(osend.at[s], orecv.at[s], recv_o.at[s])

    def attend(i, c):
        tile = ring(i)
        at = pl.ds(pl.multiple_of(tile * 256, 256), 256)
        mixed = []
        for f in range(2):
            scores = dot(k_f[f, :, :HS], q_f[f, :HS, at])
            top = jnp.max(scores, axis=0, keepdims=True) * FACTOR
            raised = jnp.exp2(scores * FACTOR - top)
            total = jnp.sum(raised, axis=0, keepdims=True)
            mix = dot(v_f[f, :HS, :], raised.astype(BF))
            mixed.append((mix / total).astype(BF))
        for m in range(2):
            back = dot(jnp.concatenate([x[:, 128 * m : 128 * m + 128] for x in mixed], axis=1), sort_t)
            for n in range(2):
                osend[4 * tile + 2 * m + n] = back[:, 128 * n : 128 * n + 128].reshape(9, 8, 128).astype(BF)
        for n in range(4):
            p = 4 * tile + line(n)

            @pl.when(p != s)
            def _():
                copy_o(p, s).start()

            @pl.when(p == s)
            def _():
                own_o.start()

        return c

    lax.fori_loop(0, 4, attend, 0)
    inputs[5].wait()

    def wait_o(p, c):
        pltpu.make_async_copy(orecv.at[p], orecv.at[p], recv_o.at[p]).wait()
        return c

    zeros = jnp.zeros((128, 128), BF)

    def pack_v(j):
        pair = []
        for n in (2 * j, 2 * j + 1):
            if n == LT:
                pair.append(zeros)
                continue
            rows = [orecv[r // 9, r % 9] for r in range(16 * n, 16 * n + 16)]
            block = dot_nt(eye, jnp.concatenate(rows, axis=0)).astype(BF)
            lanes = slice(128 * n, 128 * n + 128)
            spatial_ref[:, :, lanes] = block.reshape(2, 64, 128)
            stream = staged[5, :, :, lanes].reshape(128, 128)
            pair.append((stream.astype(F32) + block.astype(F32)).astype(BF))
        vs[:, j] = dot(to_peer, jnp.concatenate(pair, axis=0)).reshape(32, 8, 128).astype(BF)

    def unpack_v(j):
        both = dot(to_position, vr[:, j].reshape(256, 128)).astype(BF)
        for n in range(2):
            if 2 * j + n < LT:
                v_p[:, 128 * (2 * j + n) : 128 * (2 * j + n) + 128] = both[128 * n : 128 * n + 128]

    first_v, last_v = slice(0, 3), slice(3, 5)
    lax.fori_loop(0, 11, wait_o, 0)
    start_far(qks, qkr, send_qk, recv_qk, low=8)
    for j in range(3):
        pack_v(j)
    start_all(vs, vr, send_v.at[0], recv_v.at[0], first_v)
    lax.fori_loop(11, NS, wait_o, 0)
    for j in range(3, 5):
        pack_v(j)
    start_all(vs, vr, send_v.at[1], recv_v.at[1], last_v)

    store_s = pltpu.make_async_copy(spatial_ref, spatial_hbm, stores.at[0])
    store_s.start()

    to_position = one_hot(256, by_position)
    wait_tm(qkr, recv_qk)
    for j in range(LT):
        both = dot(to_position, qkr[:, j].reshape(256, 128)).astype(BF)
        q_p[:, 128 * j : 128 * j + 128] = both[:128]
        k_p[:, 128 * j : 128 * j + 128] = both[128:]

    rows = lax.broadcasted_iota(jnp.int32, (128, 128), 0)
    cols = lax.broadcasted_iota(jnp.int32, (128, 128), 1)
    same = (rows >> 6) == (cols >> 6)

    def head(h):
        low, high = HS * h // 128 * 128, -(-HS * (h + 1) // 128) * 128
        lane = lax.broadcasted_iota(jnp.int32, (128, high - low), 1) + low
        mine = (lane >= HS * h) & (lane < HS * (h + 1))
        keys = jnp.where(mine, k_p[:, low:high].astype(F32), 0.0).astype(BF)
        scores = jnp.where(same, dot_nt(q_p[:, low:high], keys), -jnp.inf)
        top = jnp.max(scores, axis=1, keepdims=True) * FACTOR
        raised = jnp.exp2(scores * FACTOR - top)
        total = jnp.sum(raised, axis=1, keepdims=True)
        mix = dot(raised.astype(BF), v_p[:, low:high]) / total
        o_p[:, low:high] = jnp.where(mine, mix, o_p[:, low:high])

    from_position = one_hot_t(256, by_position)

    def pack_t(j):
        pair = [o_p[:, 128 * n : 128 * n + 128].astype(BF) if n < LT else zeros for n in (2 * j, 2 * j + 1)]
        ts[:, j] = dot(from_position, jnp.concatenate(pair, axis=0)).reshape(32, 8, 128).astype(BF)

    first_t, last_t = slice(0, 2), slice(2, 5)
    wait_tm(vr, recv_v.at[0], first_v)
    for j in range(3):
        unpack_v(j)
    for h in range(8):
        head(h)
    for j in range(2):
        pack_t(j)
    start_all(ts, tr, send_t.at[0], recv_t.at[0], first_t)
    for h in range(8, 10):
        head(h)
    wait_tm(vr, recv_v.at[1], last_v)
    for j in range(3, 5):
        unpack_v(j)
    for h in range(10, HEADS):
        head(h)
    for j in range(2, 5):
        pack_t(j)
    start_all(ts, tr, send_t.at[1], recv_t.at[1], last_t)

    from_peer = one_hot_t(256, by_peer)

    def unpack_t(j):
        both = dot(from_peer, tr[:, j].reshape(256, 128)).astype(BF)
        for n in range(2):
            if 2 * j + n < LT:
                lanes = slice(128 * (2 * j + n), 128 * (2 * j + n) + 128)
                temporal_ref[:, :, lanes] = both[128 * n : 128 * n + 128].reshape(2, 64, 128)

    wait_tm(tr, recv_t.at[0], first_t)
    for j in range(2):
        unpack_t(j)
    store_a = pltpu.make_async_copy(
        temporal_ref.at[:, :, :512], temporal_hbm.at[:, :, :512], stores.at[1]
    )
    store_a.start()
    wait_tm(tr, recv_t.at[1], last_t)
    for j in range(2, 5):
        unpack_t(j)

    store_b = pltpu.make_async_copy(
        temporal_ref.at[:, :, 512:], temporal_hbm.at[:, :, 512:], stores.at[2]
    )
    store_b.start()

    def sent_o(i, c):
        p = lax.rem(s + i, NS)
        copy_o(p, p).wait_send()
        return c

    lax.fori_loop(1, NS, sent_o, 0)
    sent_tm(qks, send_qk)
    for n, part in enumerate((first_v, last_v)):
        sent_tm(vs, send_v.at[n], part)
    for n, part in enumerate((first_t, last_t)):
        sent_tm(ts, send_t.at[n], part)
    for copy in (store_s, store_a, store_b):
        copy.wait()


def per_device(*args):
    whole = jax.ShapeDtypeStruct((2, 64, D), BF)
    dma = pltpu.SemaphoreType.DMA
    vmem = pltpu.VMEM
    return pl.pallas_call(
        kernel,
        out_shape=(whole, whole),
        in_specs=[pl.BlockSpec(memory_space=pltpu.HBM)] * 6,
        out_specs=(pl.BlockSpec(memory_space=pltpu.HBM),) * 2,
        scratch_shapes=[
            vmem((2, 64, D), BF),
            vmem((2, 64, D), BF),
            vmem((6, 2, 64, D), BF),
            vmem((3, 144, 8, 128), BF),
            vmem((NS, 3, 9, 8, 128), BF),
            vmem((NS, 9, 8, 128), BF),
            vmem((NS, 9, 8, 128), BF),
            vmem((NT, LT, 8, 128), BF),
            vmem((NT, LT, 8, 128), BF),
            vmem((NT, 5, 8, 128), BF),
            vmem((NT, 5, 8, 128), BF),
            vmem((NT, 5, 8, 128), BF),
            vmem((NT, 5, 8, 128), BF),
            vmem((2, 80, 1024), BF),
            vmem((2, 1024, 128), BF),
            vmem((2, 80, 1024), BF),
            vmem((128, D), BF),
            vmem((128, D), BF),
            vmem((128, D), BF),
            vmem((128, D), F32),
            *[dma((NS,))] * 4,
            *[dma((NT,))] * 2,
            *[dma((2, NT))] * 4,
            dma((6,)),
            dma((3,)),
        ],
        compiler_params=pltpu.CompilerParams(
            collective_id=0, has_side_effects=True, vmem_limit_bytes=60 * 2**20
        ),
        cost_estimate=pl.CostEstimate(flops=2 * 10**9, bytes_accessed=3 * 10**6, transcendentals=3 * 10**6),
        name="attention",
    )(*args)


def solution(mesh):
    spec = P("tm", "space", None)
    return jax.shard_map(
        per_device, mesh=mesh, in_specs=(spec,) * 6, out_specs=(spec, spec), check_vma=False
    )
```
